256 devices in a mesh: row: 64 (over x, z, core), col: 4 (over y).
Axes of the slice: x: 4, y: 4, z: 8, core: 2. Of those that a mesh axis runs over, the one named last changes fastest.
Arguments:
- right_side: bfloat16 [6, 128, 256, 512], P(None, 'row'), may hold values from -6 to 6
- lower_blocks: bfloat16 [5, 128, 8, 256, 256], P(None, 'row', None, 'col'), may hold values from -0.125 to 0.125
- upper_blocks: bfloat16 [5, 128, 8, 256, 256], P(None, 'row', None, 'col'), may hold values from -0.125 to 0.125
- lower_inverse: bfloat16 [6, 128, 256, 256], P(None, 'row', 'col'), may hold values from -0.3125 to 0.3125
- upper_inverse: bfloat16 [6, 128, 256, 256], P(None, 'row', 'col'), may hold values from -0.3125 to 0.3125
- lower_source: int32 [5, 128, 8], P(None, 'row'), may hold values from 0 to 127, as said below
- upper_source: int32 [5, 128, 8], P(None, 'row'), may hold values from 0 to 127, as said below
Outputs:
- solution: bfloat16 [6, 128, 256, 512], P(None, 'row', 'col')
The draws below stay inside these ranges and needn't reach their ends.
Inputs may be any that keep to these rules, and one draw needn't show every extreme that they name: `lower_source`: each entry lies in the block of supernodes held by the same index of row as its own supernode n or by the index just before or after it: between max(0, (n // 2 - 1) * 2) and min(128, (n // 2 + 2) * 2) - 1. `upper_source`: each entry lies in the block of supernodes held by the same index of row as its own supernode n or by the index just before or after it: between max(0, (n // 2 - 1) * 2) and min(128, (n // 2 + 2) * 2) - 1.
All inputs are finite; a program needn't handle non-finite values.
Results may differ from the reference program's by a relative error of at most 0.04.
Values may be sent and summed in bfloat16 or wider, within the bound.
A program may use at most 64 MiB of HBM per device.

```python
import jax
import jax.numpy as jnp
from jax import lax

B = 256
R = 512
K = 8
LEVELS = 6
SN_DEV = 2
NODES = 128
N_COL = 4


def nearby_sources(key):
    offsets = jax.random.randint(key, (LEVELS - 1, NODES, K), -SN_DEV, 2 * SN_DEV)
    base = jnp.arange(NODES, dtype=jnp.int32) // SN_DEV * SN_DEV
    return jnp.clip(base[None, :, None] + offsets, 0, NODES - 1).astype(jnp.int32)


def draw_lower_source(key, part):
    key = jax.random.fold_in(key, 1)
    return nearby_sources(key)


def draw_upper_source(key, part):
    key = jax.random.fold_in(key, 2)
    return nearby_sources(key)


def block_scale(own_key, dims, split, low, high):
    def one(position, parts):
        draws = jax.random.uniform(jax.random.fold_in(jax.random.fold_in(own_key, 6), position), (parts,), jnp.float32, low / len(split), high / len(split))
        return jnp.repeat(jnp.exp(draws), dims[position] // parts).reshape((-1,) + (1,) * (len(dims) - position - 1))

    level = one(*split[0])
    for cut in split[1:]:
        level = level * one(*cut)
    return level


def noise(key, extent, deviation, limit, cuts=(), kind=jnp.bfloat16):
    values = jax.random.normal(key, extent, jnp.float32) * deviation
    if len(cuts) > 0:
        values = block_scale(key, extent, cuts, -0.22, 0.18) * values
    return jnp.clip(values, min=-limit, max=limit).astype(kind)


def setup_inputs(seed: int = 0) -> dict:
    key_of = jax.random.split(jax.random.key(seed), 8)
    return {
        "right_side": noise(key_of[0], (LEVELS, NODES, B, R), 1.0, 6.0, ((1, 64),)),
        "lower_blocks": noise(key_of[1], (LEVELS - 1, NODES, K, B, B), (K * B) ** -0.5, 0.125, ((1, 64), (3, 4))),
        "upper_blocks": noise(key_of[2], (LEVELS - 1, NODES, K, B, B), (K * B) ** -0.5, 0.125, ((1, 64), (3, 4))),
        "lower_inverse": noise(key_of[3], (LEVELS, NODES, B, B), (3 * B // 2) ** -0.5, 0.3125, ((1, 64), (2, 4))),
        "upper_inverse": noise(key_of[4], (LEVELS, NODES, B, B), (3 * B // 2) ** -0.5, 0.3125, ((1, 64), (2, 4))),
        "lower_source": draw_lower_source(jax.random.fold_in(key_of[7], 71), 0),
        "upper_source": draw_upper_source(jax.random.fold_in(key_of[7], 71), 0),
    }


def partial_sum(blocks, picked):
    group = B // N_COL
    left = blocks.astype(jnp.float32).reshape(K, N_COL, group, B)
    right = picked.astype(jnp.float32).reshape(K, N_COL, group, R)
    pieces = jnp.einsum("kcji,kcjr->cir", left, right, precision=lax.Precision.HIGHEST)
    rounded = lax.optimization_barrier(pieces.astype(jnp.bfloat16))
    return jnp.sum(rounded.astype(jnp.float32), axis=0)


def apply_inverse(inverse, values):
    return jnp.einsum("nij,njr->nir", inverse.astype(jnp.float32), values.astype(jnp.float32), precision=lax.Precision.HIGHEST).astype(jnp.bfloat16)


def level_sum(blocks, sources, previous):
    def one_node(pair):
        node_blocks, node_sources = pair
        return partial_sum(node_blocks, previous[node_sources.astype(jnp.int32)])

    return lax.map(one_node, (blocks, sources))


def reference(right_side, lower_blocks, upper_blocks, lower_inverse, upper_inverse, lower_source, upper_source):
    forward = [apply_inverse(lower_inverse[0], right_side[0])]
    for height in range(1, LEVELS):
        summed = level_sum(lower_blocks[height - 1], lower_source[height - 1], forward[-1])
        remain = (right_side[height].astype(jnp.float32) - summed).astype(jnp.bfloat16)
        forward.append(apply_inverse(lower_inverse[height], remain))
    current = apply_inverse(upper_inverse[LEVELS - 1], forward[LEVELS - 1])
    result = [current]
    for height in range(LEVELS - 2, -1, -1):
        summed = level_sum(upper_blocks[height], upper_source[height], current)
        remain = (forward[height].astype(jnp.float32) - summed).astype(jnp.bfloat16)
        current = apply_inverse(upper_inverse[height], remain)
        result.append(current)
    return jnp.stack(result[::-1], axis=0)
```

```python
import functools

import jax
import jax.numpy as jnp
from jax import lax
from jax.experimental import pallas as pl
from jax.experimental.pallas import tpu as pltpu
from jax.sharding import PartitionSpec as P

BF16 = jnp.bfloat16
F32 = jnp.float32
CHUNKS = 2


def dot(left, right):
    return lax.dot_general(left, right, (((1,), (0,)), ((), ())), preferred_element_type=F32)


def dot_nt(left, right):
    return lax.dot_general(left, right, (((1,), (1,)), ((), ())), preferred_element_type=F32)


def kernel(
    sizes,
    right_side,
    lower_blocks,
    upper_blocks,
    lower_inverse,
    upper_inverse,
    lower_source,
    upper_source,
    out,
    first_inverse,
    first_side,
    blocks,
    inverse,
    gathered,
    operator,
    known,
    kept,
    sent,
    received,
    halo_out,
    halo_in,
    part_out,
    part_in,
    gather_out,
    gather_in,
    first_sem,
    block_sem,
    own_sem,
    extra_sem,
    result_sem,
):
    levels, nodes, terms, part, order, rows, columns = sizes
    steps = 2 * (levels - 1)
    top = levels - 2
    wide = columns // CHUNKS
    row = lax.axis_index("row")
    col = lax.axis_index("col")
    count = lax.axis_size("row")
    ring = lax.axis_size("col")
    has_low = row > 0
    has_high = row < count - 1
    low = (row - 1, col)
    high = (row + 1, col)
    after = (row, lax.rem(col + 1, ring))
    before = (row, lax.rem(col + ring - 1, ring))
    own_rows = pl.ds(pl.multiple_of(col * part, part), part)

    load_inverse = pltpu.make_async_copy(lower_inverse.at[0], first_inverse, first_sem.at[0])
    load_side = pltpu.make_async_copy(right_side.at[0], first_side, first_sem.at[1])

    def load_blocks(step, source, level):
        return pltpu.make_async_copy(source.at[level], blocks.at[step], block_sem.at[step])

    def load_own(turn, source, level):
        return pltpu.make_async_copy(source.at[level], gathered.at[turn, :, 0], own_sem.at[turn])

    def load_extra(step, chunk):
        return pltpu.make_async_copy(
            right_side.at[step + 1, :, own_rows, pl.ds(chunk * wide, wide)],
            known.at[step, chunk, pl.ds(3 * nodes, nodes)],
            extra_sem.at[step, chunk],
        )

    all_blocks = [load_blocks(s, lower_blocks, s) for s in range(levels - 1)]
    all_blocks += [load_blocks(s, upper_blocks, steps - 1 - s) for s in range(levels - 1, steps)]
    all_own = [load_own(t, lower_inverse, t + 1) for t in range(levels - 1)]
    all_own += [load_own(t, upper_inverse, steps - t) for t in range(levels - 1, steps + 1)]
    all_extra = [load_extra(s, h) for s in range(levels - 1) for h in range(CHUNKS)]

    all_own[0].start()
    load_inverse.start()
    load_side.start()
    all_blocks[0].start()
    for copy in all_own[1:3]:
        copy.start()
    for copy in all_extra[:CHUNKS]:
        copy.start()
    all_blocks[1].start()

    barrier = pltpu.get_barrier_semaphore()
    for place in (after, before):
        pl.semaphore_signal(barrier, inc=1, device_id=place, device_id_type=pl.DeviceIdType.MESH)

    @pl.when(has_low)
    def _():
        pl.semaphore_signal(barrier, inc=1, device_id=low, device_id_type=pl.DeviceIdType.MESH)

    @pl.when(has_high)
    def _():
        pl.semaphore_signal(barrier, inc=1, device_id=high, device_id_type=pl.DeviceIdType.MESH)

    for copy in all_own[3:]:
        copy.start()
    for copy in all_extra[CHUNKS:]:
        copy.start()
    for copy in all_blocks[2:]:
        copy.start()

    line = lax.broadcasted_iota(jnp.int32, (part, order), 0)
    place = lax.broadcasted_iota(jnp.int32, (part, order), 1)
    chosen = jnp.where(place == line + col * part, 1.0, 0.0).astype(BF16)
    for node in range(nodes):
        for other in range(nodes):
            operator_rows = chosen if node == other else jnp.zeros((part, order), BF16)
            inverse[node, 3 * nodes + other] = operator_rows

    @pl.when(jnp.logical_not(has_low))
    def _():
        known[:, :, 0:nodes] = jnp.zeros((steps + 1, CHUNKS, nodes, part, wide), BF16)

    @pl.when(jnp.logical_not(has_high))
    def _():
        known[:, :, 2 * nodes : 3 * nodes] = jnp.zeros((steps + 1, CHUNKS, nodes, part, wide), BF16)

    pl.semaphore_wait(barrier, 2 + jnp.where(has_low, 1, 0) + jnp.where(has_high, 1, 0))

    def remote(source, target, out_sem, in_sem, place):
        return pltpu.make_async_remote_copy(
            src_ref=source,
            dst_ref=target,
            send_sem=out_sem,
            recv_sem=in_sem,
            device_id=place,
            device_id_type=pl.DeviceIdType.MESH,
        )

    def gather_copy(turn, which):
        source, target, place = (
            (gathered.at[turn, :, 0], gathered.at[turn, :, 3], after),
            (gathered.at[turn, :, 0], gathered.at[turn, :, 1], before),
            (gathered.at[turn, 0, 3], gathered.at[turn, 0, 2], after),
            (gathered.at[turn, 1, 1], gathered.at[turn, 1, 2], before),
        )[which]
        return remote(source, target, gather_out.at[turn, which], gather_in.at[turn, which], place)

    def halo_copy(step, chunk, side):
        source = known.at[step, chunk, pl.ds(nodes, nodes)]
        target = known.at[step, chunk, pl.ds(0 if side == 0 else 2 * nodes, nodes)]
        return remote(
            source,
            target,
            halo_out.at[step, chunk, side],
            halo_in.at[step, chunk, side],
            high if side == 0 else low,
        )

    def part_copy(step, chunk, which):
        return remote(
            sent.at[step, chunk, which],
            received.at[step, chunk, which],
            part_out.at[step, chunk, which],
            part_in.at[step, chunk, which],
            after if which % 2 == 0 else before,
        )

    def result_copy(step, chunk):
        return pltpu.make_async_copy(
            known.at[step + 1, chunk, pl.ds(nodes, nodes)],
            out.at[steps - 1 - step, :, :, pl.ds(chunk * wide, wide)],
            result_sem.at[step, chunk],
        )

    def start_gather(turn):
        pltpu.make_async_copy(
            lower_inverse.at[0], gathered.at[turn, :, 0], own_sem.at[turn]
        ).wait()
        gather_copy(turn, 0).start()
        gather_copy(turn, 1).start()

    def relay_gather(turn):
        gather_copy(turn, 0).wait_recv()
        gather_copy(turn, 2).start()
        gather_copy(turn, 1).wait_recv()
        gather_copy(turn, 3).start()

    def end_gather(turn):
        gather_copy(turn, 2).wait_recv()
        gather_copy(turn, 3).wait_recv()

    def start_halo(step, chunk):
        @pl.when(has_high)
        def _():
            halo_copy(step, chunk, 0).start()

        @pl.when(has_low)
        def _():
            halo_copy(step, chunk, 1).start()

    def end_halo(step, chunk):
        @pl.when(has_low)
        def _():
            halo_copy(step, chunk, 0).wait_recv()

        @pl.when(has_high)
        def _():
            halo_copy(step, chunk, 1).wait_recv()

    def sum_blocks(step):
        pltpu.make_async_copy(lower_blocks.at[0], blocks.at[step], block_sem.at[step]).wait()
        is_lower = step < levels - 1
        lower_level = jnp.minimum(step, levels - 2)
        upper_level = jnp.minimum(steps - 1 - step, levels - 2)
        base = (row - 1) * nodes
        tile = 16

        def one(node):
            slots = []
            for term in range(terms):
                source = jnp.where(
                    is_lower,
                    lower_source[lower_level, node, term],
                    upper_source[upper_level, node, term],
                )
                slots.append(source - base)
            for start in range(0, part, tile):
                values = [
                    blocks[step, node, term, start : start + tile, :].astype(F32)
                    for term in range(terms)
                ]
                for slot in range(3 * nodes):
                    total = jnp.zeros((tile, order), F32)
                    for term in range(terms):
                        total = total - jnp.where(slots[term] == slot, values[term], 0.0)
                    inverse[node, slot, start : start + tile, :] = total.astype(BF16)

        for node in range(nodes):
            one(node)

    def make_operator(step):
        sum_blocks(step)
        turn = step + jnp.where(step < levels - 1, 0, 1)

        @pl.when(step == top)
        def _():
            end_gather(top)
            end_gather(top + 1)
            for node in range(nodes):
                lower = jnp.concatenate(
                    [gathered[top, node, lax.rem(a - col + ring, ring)] for a in range(4)], axis=0
                )
                upper = gathered[top + 1, node].reshape(order, order)
                both = dot(upper, lower).astype(BF16)
                blocks_of = inverse[node].reshape(4 * nodes * part, order)
                operator[step, :, node] = (
                    dot_nt(both, blocks_of).astype(BF16).reshape(4, part, 4 * nodes * part)
                )

        @pl.when(step != top)
        def _():
            end_gather(turn)
            for node in range(nodes):
                blocks_of = inverse[node].reshape(4 * nodes * part, order)
                operator[step, :, node] = (
                    dot_nt(gathered[turn, node].reshape(order, order), blocks_of)
                    .astype(BF16)
                    .reshape(4, part, 4 * nodes * part)
                )

    def multiply(step, chunk):
        @pl.when(step < levels - 1)
        def _():
            pltpu.make_async_copy(
                right_side.at[1, :, own_rows, pl.ds(chunk * wide, wide)],
                known.at[step, chunk, pl.ds(3 * nodes, nodes)],
                extra_sem.at[jnp.minimum(step, levels - 2), chunk],
            ).wait()

        end_halo(step, chunk)
        values = known[step, chunk].reshape(4 * nodes * part, wide)
        far = dot(operator[step, 2].reshape(nodes * part, -1), values)
        sent[step, chunk, 0] = far[:part].astype(BF16)
        sent[step, chunk, 1] = far[part:].astype(BF16)
        part_copy(step, chunk, 0).start()
        part_copy(step, chunk, 1).start()
        near = dot(operator[step, 1].reshape(nodes * part, -1), values)
        sent[step, chunk, 2] = near[part:].astype(BF16)
        part_copy(step, chunk, 2).start()
        kept[chunk, 0] = near[:part]
        near = dot(operator[step, 3].reshape(nodes * part, -1), values)
        sent[step, chunk, 3] = near[:part].astype(BF16)
        part_copy(step, chunk, 3).start()
        kept[chunk, 1] = near[part:]
        own = dot(operator[step, 0].reshape(nodes * part, -1), values)
        kept[chunk, 2] = own[:part]
        kept[chunk, 3] = own[part:]

    def pass_on(step, chunk):
        for which in range(2):
            part_copy(step, chunk, which).wait_recv()
            sent[step, chunk, 4 + which] = (
                kept[chunk, which] + received[step, chunk, which].astype(F32)
            ).astype(BF16)
            part_copy(step, chunk, 4 + which).start()

    def finish(step, chunk):
        for which in (2, 3, 4, 5):
            part_copy(step, chunk, which).wait_recv()
        first = kept[chunk, 2] + received[step, chunk, 3].astype(F32)
        first = (first + received[step, chunk, 4].astype(F32)).astype(BF16)
        second = kept[chunk, 3] + received[step, chunk, 2].astype(F32)
        second = (second + received[step, chunk, 5].astype(F32)).astype(BF16)
        known[step + 1, chunk, nodes] = first
        known[step + 1, chunk, nodes + 1] = second

        @pl.when(step < steps - 1)
        def _():
            start_halo(step + 1, chunk)

        @pl.when(step < top)
        def _():
            known[steps - 2 - step, chunk, 3 * nodes] = first
            known[steps - 2 - step, chunk, 3 * nodes + 1] = second

        @pl.when(step >= top)
        def _():
            result_copy(step, chunk).start()

    start_gather(0)
    load_inverse.wait()
    load_side.wait()
    for chunk in range(CHUNKS):
        for node in range(nodes):
            value = dot(
                first_inverse[node], first_side[node, :, chunk * wide : (chunk + 1) * wide]
            ).astype(BF16)
            known[0, chunk, nodes + node] = value
            known[steps - 1, chunk, 3 * nodes + node] = value
        start_halo(0, chunk)
    relay_gather(0)
    start_gather(1)
    make_operator(0)

    def body(step, carry):
        multiply(step, 0)

        @pl.when(step > 0)
        def _():
            finish(step - 1, 1)

        @pl.when(step == 0)
        def _():
            relay_gather(1)
            start_gather(2)
            start_gather(3)

        @pl.when(step < steps - 1)
        def _():
            make_operator(step + 1)

        pass_on(step, 0)
        multiply(step, 1)
        finish(step, 0)

        @pl.when(step == 0)
        def _():
            relay_gather(2)

        @pl.when(step + 4 <= steps)
        def _():
            start_gather(step + 4)

        pass_on(step, 1)

        @pl.when(step + 3 <= steps)
        def _():
            relay_gather(step + 3)

        return carry

    for step in range(steps):
        body(step, 0)
    finish(steps - 1, 1)

    def drain(step, carry):
        for chunk in range(CHUNKS):
            for which in range(6):
                part_copy(step, chunk, which).wait_send()

            @pl.when(has_high)
            def _():
                halo_copy(step, chunk, 0).wait_send()

            @pl.when(has_low)
            def _():
                halo_copy(step, chunk, 1).wait_send()

            @pl.when(step >= top)
            def _():
                result_copy(step, chunk).wait()

        return carry

    lax.fori_loop(0, steps, drain, 0)

    def drain_gather(turn, carry):
        for which in range(4):
            gather_copy(turn, which).wait_send()
        return carry

    lax.fori_loop(0, steps + 1, drain_gather, 0)


def on_device(
    right_side, lower_blocks, upper_blocks, lower_inverse, upper_inverse, lower_source, upper_source
):
    levels, nodes, order, columns = right_side.shape
    terms, part = lower_blocks.shape[2:4]
    rows = nodes * part
    steps = 2 * (levels - 1)
    wide = columns // CHUNKS
    sizes = (levels, nodes, terms, part, order, rows, columns)
    anywhere = pl.BlockSpec(memory_space=pl.ANY)
    scalars = pl.BlockSpec(memory_space=pltpu.SMEM)
    dma = pltpu.SemaphoreType.DMA
    return pl.pallas_call(
        functools.partial(kernel, sizes),
        out_shape=jax.ShapeDtypeStruct((levels, nodes, part, columns), BF16),
        in_specs=[anywhere] * 5 + [scalars] * 2,
        out_specs=anywhere,
        scratch_shapes=[
            pltpu.VMEM((nodes, part, order), BF16),
            pltpu.VMEM((nodes, order, columns), BF16),
            pltpu.VMEM((steps, nodes, terms, part, order), BF16),
            pltpu.VMEM((nodes, 4 * nodes, part, order), BF16),
            pltpu.VMEM((steps + 1, nodes, 4, part, order), BF16),
            pltpu.VMEM((steps, 4, nodes, part, 4 * nodes * part), BF16),
            pltpu.VMEM((steps + 1, CHUNKS, 4 * nodes, part, wide), BF16),
            pltpu.VMEM((CHUNKS, 4, part, wide), F32),
            pltpu.VMEM((steps, CHUNKS, 6, part, wide), BF16),
            pltpu.VMEM((steps, CHUNKS, 6, part, wide), BF16),
            dma((steps + 1, CHUNKS, 2)),
            dma((steps + 1, CHUNKS, 2)),
            dma((steps, CHUNKS, 6)),
            dma((steps, CHUNKS, 6)),
            dma((steps + 1, 4)),
            dma((steps + 1, 4)),
            dma((2,)),
            dma((steps,)),
            dma((steps + 1,)),
            dma((levels - 1, CHUNKS)),
            dma((steps, CHUNKS)),
        ],
        compiler_params=pltpu.CompilerParams(
            collective_id=0, has_side_effects=True, vmem_limit_bytes=48 * 1024 * 1024
        ),
        cost_estimate=pl.CostEstimate(
            flops=4_000_000_000, bytes_accessed=10_000_000, transcendentals=0
        ),
        name="solve",
    )(
        right_side,
        lower_blocks,
        upper_blocks,
        lower_inverse,
        upper_inverse,
        lower_source,
        upper_source,
    )


def solution(mesh):
    placed = (
        P(None, "row", None, None),
        P(None, "row", None, "col", None),
        P(None, "row", None, "col", None),
        P(None, "row", "col", None),
        P(None, "row", "col", None),
        P(None, "row", None),
        P(None, "row", None),
    )
    return jax.shard_map(
        on_device,
        mesh=mesh,
        in_specs=placed,
        out_specs=P(None, "row", "col", None),
        check_vma=False,
    )
```

```python
import functools

import jax
import jax.numpy as jnp
from jax import lax
from jax.experimental import pallas as pl
from jax.experimental.pallas import tpu as pltpu
from jax.sharding import PartitionSpec as P

BF16 = jnp.bfloat16
F32 = jnp.float32
CHUNKS = 4
DIRECT = 2


def dot(left, right):
    return lax.dot_general(left, right, (((1,), (0,)), ((), ())), preferred_element_type=F32)


def dot_nt(left, right):
    return lax.dot_general(left, right, (((1,), (1,)), ((), ())), preferred_element_type=F32)


def kernel(
    sizes,
    right_side,
    lower_blocks,
    upper_blocks,
    lower_inverse,
    upper_inverse,
    lower_source,
    upper_source,
    out,
    first_inverse,
    first_side,
    blocks,
    inverse,
    gathered,
    operator,
    known,
    kept,
    sent,
    received,
    halo_out,
    halo_in,
    part_out,
    part_in,
    gather_out,
    gather_in,
    first_sem,
    block_sem,
    own_sem,
    extra_sem,
    result_sem,
):
    levels, nodes, terms, part, order, rows, columns = sizes
    steps = 2 * (levels - 1)
    top = levels - 2
    wide = columns // CHUNKS
    row = lax.axis_index("row")
    col = lax.axis_index("col")
    count = lax.axis_size("row")
    ring = lax.axis_size("col")
    has_low = row > 0
    has_high = row < count - 1
    low = (row - 1, col)
    high = (row + 1, col)
    after = (row, lax.rem(col + 1, ring))
    before = (row, lax.rem(col + ring - 1, ring))
    across = (row, lax.rem(col + 2, ring))
    peers = (across, after, before)
    own_rows = pl.ds(pl.multiple_of(col * part, part), part)

    load_inverse = pltpu.make_async_copy(lower_inverse.at[0], first_inverse, first_sem.at[0])
    load_side = pltpu.make_async_copy(right_side.at[0], first_side, first_sem.at[1])

    def load_blocks(step, source, level):
        return pltpu.make_async_copy(source.at[level], blocks.at[step], block_sem.at[step])

    def load_own(turn, source, level):
        return pltpu.make_async_copy(source.at[level], gathered.at[turn, :, 3], own_sem.at[turn])

    def load_extra(step, chunk):
        return pltpu.make_async_copy(
            right_side.at[step + 1, :, own_rows, pl.ds(chunk * wide, wide)],
            known.at[step, chunk, pl.ds(3 * nodes, nodes)],
            extra_sem.at[step, chunk],
        )

    all_blocks = [load_blocks(s, lower_blocks, s) for s in range(levels - 1)]
    all_blocks += [load_blocks(s, upper_blocks, steps - 1 - s) for s in range(levels - 1, steps)]
    all_own = [load_own(t, lower_inverse, t + 1) for t in range(levels - 1)]
    all_own += [load_own(t, upper_inverse, steps - t) for t in range(levels - 1, steps + 1)]
    all_extra = [load_extra(s, h) for s in range(levels - 1) for h in range(CHUNKS)]

    all_own[0].start()
    load_inverse.start()
    load_side.start()
    all_blocks[0].start()
    for copy in all_own[1:3]:
        copy.start()
    for copy in all_extra[:CHUNKS]:
        copy.start()
    all_blocks[1].start()

    barrier = pltpu.get_barrier_semaphore()
    for place in peers:
        pl.semaphore_signal(barrier, inc=1, device_id=place, device_id_type=pl.DeviceIdType.MESH)

    @pl.when(has_low)
    def _():
        pl.semaphore_signal(barrier, inc=1, device_id=low, device_id_type=pl.DeviceIdType.MESH)

    @pl.when(has_high)
    def _():
        pl.semaphore_signal(barrier, inc=1, device_id=high, device_id_type=pl.DeviceIdType.MESH)

    for copy in all_own[3:]:
        copy.start()
    for copy in all_extra[CHUNKS:]:
        copy.start()
    for copy in all_blocks[2:]:
        copy.start()

    line = lax.broadcasted_iota(jnp.int32, (part, order), 0)
    place = lax.broadcasted_iota(jnp.int32, (part, order), 1)
    chosen = jnp.where(place == line + col * part, 1.0, 0.0).astype(BF16)
    for node in range(nodes):
        for other in range(nodes):
            operator_rows = chosen if node == other else jnp.zeros((part, order), BF16)
            inverse[node, 3 * nodes + other] = operator_rows

    @pl.when(jnp.logical_not(has_low))
    def _():
        known[:, :, 0:nodes] = jnp.zeros((steps + 1, CHUNKS, nodes, part, wide), BF16)

    @pl.when(jnp.logical_not(has_high))
    def _():
        known[:, :, 2 * nodes : 3 * nodes] = jnp.zeros((steps + 1, CHUNKS, nodes, part, wide), BF16)

    pl.semaphore_wait(barrier, 3 + jnp.where(has_low, 1, 0) + jnp.where(has_high, 1, 0))

    def remote(source, target, out_sem, in_sem, place):
        return pltpu.make_async_remote_copy(
            src_ref=source,
            dst_ref=target,
            send_sem=out_sem,
            recv_sem=in_sem,
            device_id=place,
            device_id_type=pl.DeviceIdType.MESH,
        )

    def gather_copy(turn, which):
        source, target, place = (
            (gathered.at[turn, :, 3], gathered.at[turn, :, 2], after),
            (gathered.at[turn, :, 3], gathered.at[turn, :, 1], before),
            (gathered.at[turn, 0, 2], gathered.at[turn, 0, 0], after),
            (gathered.at[turn, 1, 1], gathered.at[turn, 1, 0], before),
            (gathered.at[turn, :, 3], gathered.at[turn, :, 0], across),
        )[which]
        return remote(source, target, gather_out.at[turn, which], gather_in.at[turn, which], place)

    def halo_copy(step, chunk, side):
        source = known.at[step, chunk, pl.ds(nodes, nodes)]
        target = known.at[step, chunk, pl.ds(0 if side == 0 else 2 * nodes, nodes)]
        return remote(
            source,
            target,
            halo_out.at[step, chunk, side],
            halo_in.at[step, chunk, side],
            high if side == 0 else low,
        )

    def part_copy(step, chunk, which):
        return remote(
            sent.at[step, chunk, which],
            received.at[step, chunk, which],
            part_out.at[step, chunk, which],
            part_in.at[step, chunk, which],
            peers[which],
        )

    def result_copy(step, chunk):
        return pltpu.make_async_copy(
            known.at[step + 1, chunk, pl.ds(nodes, nodes)],
            out.at[steps - 1 - step, :, :, pl.ds(chunk * wide, wide)],
            result_sem.at[step, chunk],
        )

    def start_gather(turn):
        pltpu.make_async_copy(
            lower_inverse.at[0], gathered.at[turn, :, 3], own_sem.at[turn]
        ).wait()
        if turn < DIRECT:
            gather_copy(turn, 4).start()
        gather_copy(turn, 0).start()
        gather_copy(turn, 1).start()

    def relay_gather(turn):
        if turn < DIRECT:
            return
        gather_copy(turn, 0).wait_recv()
        gather_copy(turn, 2).start()
        gather_copy(turn, 1).wait_recv()
        gather_copy(turn, 3).start()

    def end_gather(turn):
        for which in (0, 1, 4) if turn < DIRECT else (2, 3):
            gather_copy(turn, which).wait_recv()

    def start_halo(step, chunk):
        @pl.when(has_high)
        def _():
            halo_copy(step, chunk, 0).start()

        @pl.when(has_low)
        def _():
            halo_copy(step, chunk, 1).start()

    def end_halo(step, chunk):
        @pl.when(has_low)
        def _():
            halo_copy(step, chunk, 0).wait_recv()

        @pl.when(has_high)
        def _():
            halo_copy(step, chunk, 1).wait_recv()

    def sum_blocks(step):
        pltpu.make_async_copy(lower_blocks.at[0], blocks.at[step], block_sem.at[step]).wait()
        is_lower = step < levels - 1
        sources = lower_source if is_lower else upper_source
        level = step if is_lower else steps - 1 - step
        base = (row - 1) * nodes
        tile = 16

        def one(node):
            slots = []
            for term in range(terms):
                slots.append(sources[level, node, term] - base)
            for start in range(0, part, tile):
                values = [
                    blocks[step, node, term, start : start + tile, :].astype(F32)
                    for term in range(terms)
                ]
                for slot in range(3 * nodes):
                    total = jnp.zeros((tile, order), F32)
                    for term in range(terms):
                        total = total - jnp.where(slots[term] == slot, values[term], 0.0)
                    inverse[node, slot, start : start + tile, :] = total.astype(BF16)

        for node in range(nodes):
            one(node)

    def make_operator(step):
        sum_blocks(step)
        turn = step if step < levels - 1 else step + 1
        end_gather(turn)
        if step == top:
            end_gather(top + 1)
        for node in range(nodes):
            left = gathered[turn, node].reshape(order, order)
            if step == top:
                places = [lax.rem(a - col + ring, ring) for a in range(4)]
                slots = [
                    jnp.where(p == 0, 3, jnp.where(p == 1, 1, jnp.where(p == 2, 0, 2)))
                    for p in places
                ]
                lower = jnp.concatenate([gathered[top, node, p] for p in slots], axis=0)
                upper = gathered[top + 1, node].reshape(order, order)
                left = dot(upper, lower).astype(BF16)
            right = inverse[node].reshape(4 * nodes * part, order)
            operator[step, :, node] = (
                dot_nt(left, right).astype(BF16).reshape(4, part, 4 * nodes * part)
            )

    def multiply(step, chunk):
        if step < levels - 1:
            load_extra(step, chunk).wait()
        end_halo(step, chunk)
        values = known[step, chunk].reshape(4 * nodes * part, wide)
        half = 2 * nodes * part
        one = dot(operator[step, 0:2].reshape(half, -1), values)
        sent[step, chunk, 0:2] = one.astype(BF16).reshape(2, nodes, part, wide)
        part_copy(step, chunk, 0).start()
        part_copy(step, chunk, 1).start()
        two = dot(operator[step, 2:4].reshape(half, -1), values)
        sent[step, chunk, 2] = two[: nodes * part].astype(BF16).reshape(nodes, part, wide)
        part_copy(step, chunk, 2).start()
        kept[chunk] = two[nodes * part :].reshape(nodes, part, wide)

    def finish(step, chunk):
        total = kept[chunk]
        for which in (1, 2, 0):
            part_copy(step, chunk, which).wait_recv()
        for which in range(3):
            total = total + received[step, chunk, which].astype(F32)
        value = total.astype(BF16)
        known[step + 1, chunk, nodes : 2 * nodes] = value
        if step < steps - 1:
            start_halo(step + 1, chunk)
        if step < top:
            known[steps - 2 - step, chunk, 3 * nodes :] = value
        if step >= top:
            result_copy(step, chunk).start()

    start_gather(0)
    load_inverse.wait()
    load_side.wait()
    for chunk in range(CHUNKS):
        for node in range(nodes):
            value = dot(
                first_inverse[node], first_side[node, :, chunk * wide : (chunk + 1) * wide]
            ).astype(BF16)
            known[0, chunk, nodes + node] = value
            known[steps - 1, chunk, 3 * nodes + node] = value
        start_halo(0, chunk)
    relay_gather(0)
    start_gather(1)
    make_operator(0)

    late = CHUNKS // 2
    for step in range(steps):
        for chunk in range(CHUNKS):
            multiply(step, chunk)
            if chunk < late:
                if step > 0:
                    finish(step - 1, late + chunk)
            else:
                finish(step, chunk - late)
            if chunk == 0 and step == 0:
                start_gather(2)
                start_gather(3)
            if chunk == late - 1 and step < steps - 1:
                make_operator(step + 1)
            if chunk == late and step + 3 <= steps:
                relay_gather(step + 3)
                if step == 0:
                    relay_gather(2)
        if step + 4 <= steps:
            start_gather(step + 4)
    for chunk in range(late, CHUNKS):
        finish(steps - 1, chunk)

    for step in range(steps):
        for chunk in range(CHUNKS):
            for which in range(3):
                part_copy(step, chunk, which).wait_send()
            if step >= top:
                result_copy(step, chunk).wait()

    @pl.when(has_high)
    def _():
        for step in range(steps):
            for chunk in range(CHUNKS):
                halo_copy(step, chunk, 0).wait_send()

    @pl.when(has_low)
    def _():
        for step in range(steps):
            for chunk in range(CHUNKS):
                halo_copy(step, chunk, 1).wait_send()

    for turn in range(steps + 1):
        for which in (0, 1, 4) if turn < DIRECT else (0, 1, 2, 3):
            gather_copy(turn, which).wait_send()


def on_device(
    right_side, lower_blocks, upper_blocks, lower_inverse, upper_inverse, lower_source, upper_source
):
    levels, nodes, order, columns = right_side.shape
    terms, part = lower_blocks.shape[2:4]
    rows = nodes * part
    steps = 2 * (levels - 1)
    wide = columns // CHUNKS
    sizes = (levels, nodes, terms, part, order, rows, columns)
    anywhere = pl.BlockSpec(memory_space=pl.ANY)
    scalars = pl.BlockSpec(memory_space=pltpu.SMEM)
    dma = pltpu.SemaphoreType.DMA
    return pl.pallas_call(
        functools.partial(kernel, sizes),
        out_shape=jax.ShapeDtypeStruct((levels, nodes, part, columns), BF16),
        in_specs=[anywhere] * 5 + [scalars] * 2,
        out_specs=anywhere,
        scratch_shapes=[
            pltpu.VMEM((nodes, part, order), BF16),
            pltpu.VMEM((nodes, order, columns), BF16),
            pltpu.VMEM((steps, nodes, terms, part, order), BF16),
            pltpu.VMEM((nodes, 4 * nodes, part, order), BF16),
            pltpu.VMEM((steps + 1, nodes, 4, part, order), BF16),
            pltpu.VMEM((steps, 4, nodes, part, 4 * nodes * part), BF16),
            pltpu.VMEM((steps + 1, CHUNKS, 4 * nodes, part, wide), BF16),
            pltpu.VMEM((CHUNKS, nodes, part, wide), F32),
            pltpu.VMEM((steps, CHUNKS, 3, nodes, part, wide), BF16),
            pltpu.VMEM((steps, CHUNKS, 3, nodes, part, wide), BF16),
            dma((steps + 1, CHUNKS, 2)),
            dma((steps + 1, CHUNKS, 2)),
            dma((steps, CHUNKS, 3)),
            dma((steps, CHUNKS, 3)),
            dma((steps + 1, 5)),
            dma((steps + 1, 5)),
            dma((2,)),
            dma((steps,)),
            dma((steps + 1,)),
            dma((levels - 1, CHUNKS)),
            dma((steps, CHUNKS)),
        ],
        compiler_params=pltpu.CompilerParams(
            collective_id=0, has_side_effects=True, vmem_limit_bytes=62 * 1024 * 1024
        ),
        cost_estimate=pl.CostEstimate(
            flops=4_000_000_000, bytes_accessed=10_000_000, transcendentals=0
        ),
        name="solve",
    )(
        right_side,
        lower_blocks,
        upper_blocks,
        lower_inverse,
        upper_inverse,
        lower_source,
        upper_source,
    )


def solution(mesh):
    placed = (
        P(None, "row", None, None),
        P(None, "row", None, "col", None),
        P(None, "row", None, "col", None),
        P(None, "row", "col", None),
        P(None, "row", "col", None),
        P(None, "row", None),
        P(None, "row", None),
    )
    return jax.shard_map(
        on_device,
        mesh=mesh,
        in_specs=placed,
        out_specs=P(None, "row", "col", None),
        check_vma=False,
    )
```

```python
import functools

import jax
import jax.numpy as jnp
from jax import lax
from jax.experimental import pallas as pl
from jax.experimental.pallas import tpu as pltpu
from jax.sharding import PartitionSpec as P

BF16 = jnp.bfloat16
F32 = jnp.float32
CHUNKS = 4
DIRECT = 2


def dot(left, right):
    return lax.dot_general(left, right, (((1,), (0,)), ((), ())), preferred_element_type=F32)


def dot_nt(left, right):
    return lax.dot_general(left, right, (((1,), (1,)), ((), ())), preferred_element_type=F32)


def kernel(
    sizes,
    right_side,
    lower_blocks,
    upper_blocks,
    lower_inverse,
    upper_inverse,
    lower_source,
    upper_source,
    out,
    first_inverse,
    first_side,
    blocks,
    inverse,
    gathered,
    operator,
    known,
    kept,
    sent,
    received,
    halo_out,
    halo_in,
    part_out,
    part_in,
    gather_out,
    gather_in,
    first_sem,
    block_sem,
    own_sem,
    extra_sem,
    result_sem,
):
    levels, nodes, terms, part, order, rows, columns = sizes
    steps = 2 * (levels - 1)
    top = levels - 2
    wide = columns // CHUNKS
    row = lax.axis_index("row")
    col = lax.axis_index("col")
    count = lax.axis_size("row")
    ring = lax.axis_size("col")
    has_low = row > 0
    has_high = row < count - 1
    low = (row - 1, col)
    high = (row + 1, col)
    after = (row, lax.rem(col + 1, ring))
    before = (row, lax.rem(col + ring - 1, ring))
    across = (row, lax.rem(col + 2, ring))
    peers = (across, after, before)
    own_rows = pl.ds(pl.multiple_of(col * part, part), part)

    load_inverse = pltpu.make_async_copy(lower_inverse.at[0], first_inverse, first_sem.at[0])
    load_side = pltpu.make_async_copy(right_side.at[0], first_side, first_sem.at[1])

    def load_blocks(step, source, level):
        return pltpu.make_async_copy(source.at[level], blocks.at[step], block_sem.at[step])

    def load_own(turn, source, level):
        return pltpu.make_async_copy(source.at[level], gathered.at[turn, :, 3], own_sem.at[turn])

    def load_extra(step, chunk):
        return pltpu.make_async_copy(
            right_side.at[step + 1, :, own_rows, pl.ds(chunk * wide, wide)],
            known.at[step, chunk, pl.ds(3 * nodes, nodes)],
            extra_sem.at[step, chunk],
        )

    all_blocks = [load_blocks(s, lower_blocks, s) for s in range(levels - 1)]
    all_blocks += [load_blocks(s, upper_blocks, steps - 1 - s) for s in range(levels - 1, steps)]
    all_own = [load_own(t, lower_inverse, t + 1) for t in range(levels - 1)]
    all_own += [load_own(t, upper_inverse, steps - t) for t in range(levels - 1, steps + 1)]
    all_extra = [load_extra(s, h) for s in range(levels - 1) for h in range(CHUNKS)]

    barrier = pltpu.get_barrier_semaphore()
    for place in peers:
        pl.semaphore_signal(barrier, inc=1, device_id=place, device_id_type=pl.DeviceIdType.MESH)

    @pl.when(has_low)
    def _():
        pl.semaphore_signal(barrier, inc=1, device_id=low, device_id_type=pl.DeviceIdType.MESH)

    @pl.when(has_high)
    def _():
        pl.semaphore_signal(barrier, inc=1, device_id=high, device_id_type=pl.DeviceIdType.MESH)

    all_own[0].start()
    load_inverse.start()
    load_side.start()
    all_blocks[0].start()
    all_own[1].start()

    line = lax.broadcasted_iota(jnp.int32, (part, order), 0)
    place = lax.broadcasted_iota(jnp.int32, (part, order), 1)
    chosen = jnp.where(place == line + col * part, 1.0, 0.0).astype(BF16)
    for node in range(nodes):
        for other in range(nodes):
            operator_rows = chosen if node == other else jnp.zeros((part, order), BF16)
            inverse[node, 3 * nodes + other] = operator_rows

    @pl.when(jnp.logical_not(has_low))
    def _():
        known[:, :, 0:nodes] = jnp.zeros((steps + 1, CHUNKS, nodes, part, wide), BF16)

    @pl.when(jnp.logical_not(has_high))
    def _():
        known[:, :, nodes : 2 * nodes] = jnp.zeros((steps + 1, CHUNKS, nodes, part, wide), BF16)

    pl.semaphore_wait(barrier, 3 + jnp.where(has_low, 1, 0) + jnp.where(has_high, 1, 0))

    def remote(source, target, out_sem, in_sem, place):
        return pltpu.make_async_remote_copy(
            src_ref=source,
            dst_ref=target,
            send_sem=out_sem,
            recv_sem=in_sem,
            device_id=place,
            device_id_type=pl.DeviceIdType.MESH,
        )

    def gather_copy(turn, which):
        source, target, place = (
            (gathered.at[turn, :, 3], gathered.at[turn, :, 2], after),
            (gathered.at[turn, :, 3], gathered.at[turn, :, 1], before),
            (gathered.at[turn, 0, 2], gathered.at[turn, 0, 0], after),
            (gathered.at[turn, 1, 1], gathered.at[turn, 1, 0], before),
            (gathered.at[turn, :, 3], gathered.at[turn, :, 0], across),
        )[which]
        return remote(source, target, gather_out.at[turn, which], gather_in.at[turn, which], place)

    def halo_copy(step, chunk, side):
        source = known.at[step, chunk, pl.ds(2 * nodes, nodes)]
        target = known.at[step, chunk, pl.ds(0 if side == 0 else nodes, nodes)]
        return remote(
            source,
            target,
            halo_out.at[step, chunk, side],
            halo_in.at[step, chunk, side],
            high if side == 0 else low,
        )

    def part_copy(step, chunk, which):
        return remote(
            sent.at[step, chunk, which],
            received.at[step, chunk, which],
            part_out.at[step, chunk, which],
            part_in.at[step, chunk, which],
            peers[which],
        )

    def result_copy(step, chunk):
        return pltpu.make_async_copy(
            known.at[step + 1, chunk, pl.ds(2 * nodes, nodes)],
            out.at[steps - 1 - step, :, :, pl.ds(chunk * wide, wide)],
            result_sem.at[step, chunk],
        )

    def start_gather(turn):
        pltpu.make_async_copy(
            lower_inverse.at[0], gathered.at[turn, :, 3], own_sem.at[turn]
        ).wait()
        if turn < DIRECT:
            gather_copy(turn, 4).start()
        gather_copy(turn, 0).start()
        gather_copy(turn, 1).start()

    def relay_gather(turn):
        if turn < DIRECT:
            return
        gather_copy(turn, 0).wait_recv()
        gather_copy(turn, 2).start()
        gather_copy(turn, 1).wait_recv()
        gather_copy(turn, 3).start()

    def end_gather(turn):
        for which in (0, 1, 4) if turn < DIRECT else (2, 3):
            gather_copy(turn, which).wait_recv()

    def start_halo(step, chunk):
        @pl.when(has_high)
        def _():
            halo_copy(step, chunk, 0).start()

        @pl.when(has_low)
        def _():
            halo_copy(step, chunk, 1).start()

    def end_halo(step, chunk):
        @pl.when(has_low)
        def _():
            halo_copy(step, chunk, 0).wait_recv()

        @pl.when(has_high)
        def _():
            halo_copy(step, chunk, 1).wait_recv()

    def sum_blocks(step):
        pltpu.make_async_copy(lower_blocks.at[0], blocks.at[step], block_sem.at[step]).wait()
        is_lower = step < levels - 1
        sources = lower_source if is_lower else upper_source
        level = step if is_lower else steps - 1 - step
        base = (row - 1) * nodes
        spots = [*range(nodes), *range(2 * nodes, 3 * nodes), *range(nodes, 2 * nodes)]
        tile = 16

        def one(node):
            slots = []
            for term in range(terms):
                slots.append(sources[level, node, term] - base)
            for start in range(0, part, tile):
                values = [
                    blocks[step, node, term, start : start + tile, :].astype(F32)
                    for term in range(terms)
                ]
                for slot in range(3 * nodes):
                    total = jnp.zeros((tile, order), F32)
                    for term in range(terms):
                        total = total - jnp.where(slots[term] == slot, values[term], 0.0)
                    inverse[node, spots[slot], start : start + tile, :] = total.astype(BF16)

        for node in range(nodes):
            one(node)

    def make_operator(step):
        sum_blocks(step)
        turn = step if step < levels - 1 else step + 1
        end_gather(turn)
        if step == top:
            end_gather(top + 1)
        for node in range(nodes):
            left = gathered[turn, node].reshape(order, order)
            if step == top:
                places = [lax.rem(a - col + ring, ring) for a in range(4)]
                slots = [
                    jnp.where(p == 0, 3, jnp.where(p == 1, 1, jnp.where(p == 2, 0, 2)))
                    for p in places
                ]
                lower = jnp.concatenate([gathered[top, node, p] for p in slots], axis=0)
                upper = gathered[top + 1, node].reshape(order, order)
                left = dot(upper, lower).astype(BF16)
            right = inverse[node].reshape(4 * nodes * part, order)
            operator[step, :, node] = (
                dot_nt(left, right).astype(BF16).reshape(4, part, 4 * nodes * part)
            )

    def multiply(step, chunk):
        if step < levels - 1:
            load_extra(step, chunk).wait()
        half = 2 * nodes * part
        near = known[step, chunk, 2 * nodes :].reshape(half, wide)
        one = dot(operator[step, 0:2, :, :, half:].reshape(half, half), near)
        two = dot(operator[step, 2:4, :, :, half:].reshape(half, half), near)
        end_halo(step, chunk)
        far = known[step, chunk, : 2 * nodes].reshape(half, wide)
        one = one + dot(operator[step, 0:2, :, :, :half].reshape(half, half), far)
        sent[step, chunk, 0:2] = one.astype(BF16).reshape(2, nodes, part, wide)
        part_copy(step, chunk, 0).start()
        part_copy(step, chunk, 1).start()
        two = two + dot(operator[step, 2:4, :, :, :half].reshape(half, half), far)
        sent[step, chunk, 2] = two[: nodes * part].astype(BF16).reshape(nodes, part, wide)
        part_copy(step, chunk, 2).start()
        kept[chunk] = two[nodes * part :].reshape(nodes, part, wide)

    def finish(step, chunk):
        total = kept[chunk]
        for which in (1, 2, 0):
            part_copy(step, chunk, which).wait_recv()
        for which in range(3):
            total = total + received[step, chunk, which].astype(F32)
        value = total.astype(BF16)
        known[step + 1, chunk, 2 * nodes : 3 * nodes] = value
        if step < steps - 1:
            start_halo(step + 1, chunk)
        if step < top:
            known[steps - 2 - step, chunk, 3 * nodes :] = value
        if step >= top:
            result_copy(step, chunk).start()

    start_gather(0)
    for copy in all_extra[:CHUNKS]:
        copy.start()
    load_inverse.wait()
    load_side.wait()
    for chunk in range(CHUNKS):
        for node in range(nodes):
            value = dot(
                first_inverse[node], first_side[node, :, chunk * wide : (chunk + 1) * wide]
            ).astype(BF16)
            known[0, chunk, 2 * nodes + node] = value
            known[steps - 1, chunk, 3 * nodes + node] = value
        start_halo(0, chunk)
    start_gather(1)
    for copy in (*all_own[2:4], all_blocks[1], *all_extra[CHUNKS:2 * CHUNKS]):
        copy.start()
    make_operator(0)
    for copy in (*all_own[4:], *all_blocks[2:], *all_extra[2 * CHUNKS:]):
        copy.start()

    late = CHUNKS // 2
    for step in range(steps):
        for chunk in range(CHUNKS):
            multiply(step, chunk)
            if chunk < late:
                if step > 0:
                    finish(step - 1, late + chunk)
            else:
                finish(step, chunk - late)
            if chunk == 0 and step == 0:
                start_gather(2)
                start_gather(3)
            if chunk == late - 1 and step < steps - 1:
                make_operator(step + 1)
            if chunk == late and step + 3 <= steps:
                relay_gather(step + 3)
                if step == 0:
                    relay_gather(2)
        if step + 4 <= steps:
            start_gather(step + 4)
    for chunk in range(late, CHUNKS):
        finish(steps - 1, chunk)

    for step in range(steps):
        for chunk in range(CHUNKS):
            for which in range(3):
                part_copy(step, chunk, which).wait_send()
            if step >= top:
                result_copy(step, chunk).wait()

    @pl.when(has_high)
    def _():
        for step in range(steps):
            for chunk in range(CHUNKS):
                halo_copy(step, chunk, 0).wait_send()

    @pl.when(has_low)
    def _():
        for step in range(steps):
            for chunk in range(CHUNKS):
                halo_copy(step, chunk, 1).wait_send()

    for turn in range(steps + 1):
        for which in (0, 1, 4) if turn < DIRECT else (0, 1, 2, 3):
            gather_copy(turn, which).wait_send()


def on_device(
    right_side, lower_blocks, upper_blocks, lower_inverse, upper_inverse, lower_source, upper_source
):
    levels, nodes, order, columns = right_side.shape
    terms, part = lower_blocks.shape[2:4]
    rows = nodes * part
    steps = 2 * (levels - 1)
    wide = columns // CHUNKS
    sizes = (levels, nodes, terms, part, order, rows, columns)
    anywhere = pl.BlockSpec(memory_space=pl.ANY)
    scalars = pl.BlockSpec(memory_space=pltpu.SMEM)
    dma = pltpu.SemaphoreType.DMA
    return pl.pallas_call(
        functools.partial(kernel, sizes),
        out_shape=jax.ShapeDtypeStruct((levels, nodes, part, columns), BF16),
        in_specs=[anywhere] * 5 + [scalars] * 2,
        out_specs=anywhere,
        scratch_shapes=[
            pltpu.VMEM((nodes, part, order), BF16),
            pltpu.VMEM((nodes, order, columns), BF16),
            pltpu.VMEM((steps, nodes, terms, part, order), BF16),
            pltpu.VMEM((nodes, 4 * nodes, part, order), BF16),
            pltpu.VMEM((steps + 1, nodes, 4, part, order), BF16),
            pltpu.VMEM((steps, 4, nodes, part, 4 * nodes * part), BF16),
            pltpu.VMEM((steps + 1, CHUNKS, 4 * nodes, part, wide), BF16),
            pltpu.VMEM((CHUNKS, nodes, part, wide), F32),
            pltpu.VMEM((steps, CHUNKS, 3, nodes, part, wide), BF16),
            pltpu.VMEM((steps, CHUNKS, 3, nodes, part, wide), BF16),
            dma((steps + 1, CHUNKS, 2)),
            dma((steps + 1, CHUNKS, 2)),
            dma((steps, CHUNKS, 3)),
            dma((steps, CHUNKS, 3)),
            dma((steps + 1, 5)),
            dma((steps + 1, 5)),
            dma((2,)),
            dma((steps,)),
            dma((steps + 1,)),
            dma((levels - 1, CHUNKS)),
            dma((steps, CHUNKS)),
        ],
        compiler_params=pltpu.CompilerParams(
            collective_id=0, has_side_effects=True, vmem_limit_bytes=62 * 1024 * 1024
        ),
        cost_estimate=pl.CostEstimate(
            flops=4_000_000_000, bytes_accessed=10_000_000, transcendentals=0
        ),
        name="solve",
    )(
        right_side,
        lower_blocks,
        upper_blocks,
        lower_inverse,
        upper_inverse,
        lower_source,
        upper_source,
    )


def solution(mesh):
    placed = (
        P(None, "row", None, None),
        P(None, "row", None, "col", None),
        P(None, "row", None, "col", None),
        P(None, "row", "col", None),
        P(None, "row", "col", None),
        P(None, "row", None),
        P(None, "row", None),
    )
    return jax.shard_map(
        on_device,
        mesh=mesh,
        in_specs=placed,
        out_specs=P(None, "row", "col", None),
        check_vma=False,
    )
```

```python
import functools

import jax
import jax.numpy as jnp
from jax import lax
from jax.experimental import pallas as pl
from jax.experimental.pallas import tpu as pltpu
from jax.sharding import PartitionSpec as P

BF16 = jnp.bfloat16
F32 = jnp.float32
CHUNKS = 4
DIRECT = 2


def dot(left, right):
    return lax.dot_general(left, right, (((1,), (0,)), ((), ())), preferred_element_type=F32)


def dot_nt(left, right):
    return lax.dot_general(left, right, (((1,), (1,)), ((), ())), preferred_element_type=F32)


def kernel(
    sizes,
    right_side,
    lower_blocks,
    upper_blocks,
    lower_inverse,
    upper_inverse,
    lower_source,
    upper_source,
    out,
    first_inverse,
    first_side,
    blocks,
    inverse,
    gathered,
    operator,
    known,
    kept,
    sent,
    received,
    halo_out,
    halo_in,
    part_out,
    part_in,
    gather_out,
    gather_in,
    first_sem,
    block_sem,
    own_sem,
    extra_sem,
    result_sem,
):
    levels, nodes, terms, part, order, rows, columns = sizes
    steps = 2 * (levels - 1)
    top = levels - 2
    wide = columns // CHUNKS
    row = lax.axis_index("row")
    col = lax.axis_index("col")
    count = lax.axis_size("row")
    ring = lax.axis_size("col")
    has_low = row > 0
    has_high = row < count - 1
    low = (row - 1, col)
    high = (row + 1, col)
    after = (row, lax.rem(col + 1, ring))
    before = (row, lax.rem(col + ring - 1, ring))
    across = (row, lax.rem(col + 2, ring))
    peers = (across, after, before)
    own_rows = pl.ds(pl.multiple_of(col * part, part), part)

    load_inverse = pltpu.make_async_copy(lower_inverse.at[0], first_inverse, first_sem.at[0])
    load_side = pltpu.make_async_copy(right_side.at[0], first_side, first_sem.at[1])

    def load_blocks(step, source, level):
        return pltpu.make_async_copy(source.at[level], blocks.at[step], block_sem.at[step])

    def load_own(turn, source, level):
        return pltpu.make_async_copy(source.at[level], gathered.at[turn, :, 3], own_sem.at[turn])

    def load_extra(step, chunk):
        return pltpu.make_async_copy(
            right_side.at[step + 1, :, own_rows, pl.ds(chunk * wide, wide)],
            known.at[step, chunk, pl.ds(3 * nodes, nodes)],
            extra_sem.at[step, chunk],
        )

    all_blocks = [load_blocks(s, lower_blocks, s) for s in range(levels - 1)]
    all_blocks += [load_blocks(s, upper_blocks, steps - 1 - s) for s in range(levels - 1, steps)]
    all_own = [load_own(t, lower_inverse, t + 1) for t in range(levels - 1)]
    all_own += [load_own(t, upper_inverse, steps - t) for t in range(levels - 1, steps + 1)]
    all_extra = [load_extra(s, h) for s in range(levels - 1) for h in range(CHUNKS)]

    barrier = pltpu.get_barrier_semaphore()
    for place in peers:
        pl.semaphore_signal(barrier, inc=1, device_id=place, device_id_type=pl.DeviceIdType.MESH)

    @pl.when(has_low)
    def _():
        pl.semaphore_signal(barrier, inc=1, device_id=low, device_id_type=pl.DeviceIdType.MESH)

    @pl.when(has_high)
    def _():
        pl.semaphore_signal(barrier, inc=1, device_id=high, device_id_type=pl.DeviceIdType.MESH)

    all_own[0].start()
    load_inverse.start()
    load_side.start()
    all_blocks[0].start()
    all_own[1].start()

    line = lax.broadcasted_iota(jnp.int32, (part, order), 0)
    place = lax.broadcasted_iota(jnp.int32, (part, order), 1)
    chosen = jnp.where(place == line + col * part, 1.0, 0.0).astype(BF16)
    for node in range(nodes):
        for other in range(nodes):
            operator_rows = chosen if node == other else jnp.zeros((part, order), BF16)
            inverse[node, 3 * nodes + other] = operator_rows

    @pl.when(jnp.logical_not(has_low))
    def _():
        known[:, :, 0:nodes] = jnp.zeros((steps + 1, CHUNKS, nodes, part, wide), BF16)

    @pl.when(jnp.logical_not(has_high))
    def _():
        known[:, :, nodes : 2 * nodes] = jnp.zeros((steps + 1, CHUNKS, nodes, part, wide), BF16)

    pl.semaphore_wait(barrier, 3 + jnp.where(has_low, 1, 0) + jnp.where(has_high, 1, 0))

    def remote(source, target, out_sem, in_sem, place):
        return pltpu.make_async_remote_copy(
            src_ref=source,
            dst_ref=target,
            send_sem=out_sem,
            recv_sem=in_sem,
            device_id=place,
            device_id_type=pl.DeviceIdType.MESH,
        )

    def gather_copy(turn, which):
        source, target, place = (
            (gathered.at[turn, :, 3], gathered.at[turn, :, 2], after),
            (gathered.at[turn, :, 3], gathered.at[turn, :, 1], before),
            (gathered.at[turn, 0, 2], gathered.at[turn, 0, 0], after),
            (gathered.at[turn, 1, 1], gathered.at[turn, 1, 0], before),
            (gathered.at[turn, :, 3], gathered.at[turn, :, 0], across),
        )[which]
        return remote(source, target, gather_out.at[turn, which], gather_in.at[turn, which], place)

    def halo_copy(step, chunk, side):
        source = known.at[step, chunk, pl.ds(2 * nodes, nodes)]
        target = known.at[step, chunk, pl.ds(0 if side == 0 else nodes, nodes)]
        return remote(
            source,
            target,
            halo_out.at[step, chunk, side],
            halo_in.at[step, chunk, side],
            high if side == 0 else low,
        )

    def part_copy(step, chunk, which):
        return remote(
            sent.at[step, chunk, which],
            received.at[step, chunk, which],
            part_out.at[step, chunk, which],
            part_in.at[step, chunk, which],
            peers[which],
        )

    def result_copy(step, chunk):
        return pltpu.make_async_copy(
            known.at[step + 1, chunk, pl.ds(2 * nodes, nodes)],
            out.at[steps - 1 - step, :, :, pl.ds(chunk * wide, wide)],
            result_sem.at[step, chunk],
        )

    def start_gather(turn):
        pltpu.make_async_copy(
            lower_inverse.at[0], gathered.at[turn, :, 3], own_sem.at[turn]
        ).wait()
        if turn < DIRECT:
            gather_copy(turn, 4).start()
        gather_copy(turn, 0).start()
        gather_copy(turn, 1).start()

    def relay_gather(turn):
        if turn < DIRECT:
            return
        gather_copy(turn, 0).wait_recv()
        gather_copy(turn, 2).start()
        gather_copy(turn, 1).wait_recv()
        gather_copy(turn, 3).start()

    def end_gather(turn):
        for which in (0, 1, 4) if turn < DIRECT else (2, 3):
            gather_copy(turn, which).wait_recv()

    def start_halo(step, chunk):
        @pl.when(has_high)
        def _():
            halo_copy(step, chunk, 0).start()

        @pl.when(has_low)
        def _():
            halo_copy(step, chunk, 1).start()

    def end_halo(step, chunk):
        @pl.when(has_low)
        def _():
            halo_copy(step, chunk, 0).wait_recv()

        @pl.when(has_high)
        def _():
            halo_copy(step, chunk, 1).wait_recv()

    def sum_blocks(step):
        pltpu.make_async_copy(lower_blocks.at[0], blocks.at[step], block_sem.at[step]).wait()
        is_lower = step < levels - 1
        sources = lower_source if is_lower else upper_source
        level = step if is_lower else steps - 1 - step
        base = (row - 1) * nodes
        spots = [*range(nodes), *range(2 * nodes, 3 * nodes), *range(nodes, 2 * nodes)]
        tile = 16

        def one(node):
            slots = []
            for term in range(terms):
                slots.append(sources[level, node, term] - base)
            for start in range(0, part, tile):
                values = [
                    blocks[step, node, term, start : start + tile, :].astype(F32)
                    for term in range(terms)
                ]
                for slot in range(3 * nodes):
                    total = jnp.zeros((tile, order), F32)
                    for term in range(terms):
                        total = total - jnp.where(slots[term] == slot, values[term], 0.0)
                    inverse[node, spots[slot], start : start + tile, :] = total.astype(BF16)

        for node in range(nodes):
            one(node)

    def make_operator(step):
        sum_blocks(step)
        turn = step if step < levels - 1 else step + 1
        end_gather(turn)
        if step == top:
            end_gather(top + 1)
        for node in range(nodes):
            left = gathered[turn, node].reshape(order, order)
            if step == top:
                places = [lax.rem(a - col + ring, ring) for a in range(4)]
                slots = [
                    jnp.where(p == 0, 3, jnp.where(p == 1, 1, jnp.where(p == 2, 0, 2)))
                    for p in places
                ]
                lower = jnp.concatenate([gathered[top, node, p] for p in slots], axis=0)
                upper = gathered[top + 1, node].reshape(order, order)
                left = dot(upper, lower).astype(BF16)
            right = inverse[node].reshape(4 * nodes * part, order)
            operator[step, :, node] = (
                dot_nt(left, right).astype(BF16).reshape(4, part, 4 * nodes * part)
            )

    def multiply(step, chunk):
        if step < levels - 1:
            load_extra(step, chunk).wait()
        half = 2 * nodes * part
        near = known[step, chunk, 2 * nodes :].reshape(half, wide)
        one = dot(operator[step, 0:2, :, :, half:].reshape(half, half), near)
        two = dot(operator[step, 2:4, :, :, half:].reshape(half, half), near)
        end_halo(step, chunk)
        far = known[step, chunk, : 2 * nodes].reshape(half, wide)
        one = one + dot(operator[step, 0:2, :, :, :half].reshape(half, half), far)
        sent[step, chunk, 0:2] = one.astype(BF16).reshape(2, nodes, part, wide)
        part_copy(step, chunk, 0).start()
        part_copy(step, chunk, 1).start()
        two = two + dot(operator[step, 2:4, :, :, :half].reshape(half, half), far)
        sent[step, chunk, 2] = two[: nodes * part].astype(BF16).reshape(nodes, part, wide)
        part_copy(step, chunk, 2).start()
        kept[chunk] = two[nodes * part :].reshape(nodes, part, wide)

    def finish(step, chunk):
        total = kept[chunk]
        for which in (1, 2, 0):
            part_copy(step, chunk, which).wait_recv()
            total = total + received[step, chunk, which].astype(F32)
        value = total.astype(BF16)
        known[step + 1, chunk, 2 * nodes : 3 * nodes] = value
        if step < steps - 1:
            start_halo(step + 1, chunk)
        if step < top:
            known[steps - 2 - step, chunk, 3 * nodes :] = value
        if step >= top:
            result_copy(step, chunk).start()

    start_gather(0)
    for copy in all_extra[:CHUNKS]:
        copy.start()
    load_inverse.wait()
    load_side.wait()
    for chunk in range(CHUNKS):
        for node in range(nodes):
            value = dot(
                first_inverse[node], first_side[node, :, chunk * wide : (chunk + 1) * wide]
            ).astype(BF16)
            known[0, chunk, 2 * nodes + node] = value
            known[steps - 1, chunk, 3 * nodes + node] = value
        start_halo(0, chunk)
    start_gather(1)
    for copy in (*all_own[2:4], all_blocks[1], *all_extra[CHUNKS:2 * CHUNKS]):
        copy.start()
    make_operator(0)
    for copy in (*all_own[4:], *all_blocks[2:], *all_extra[2 * CHUNKS:]):
        copy.start()

    late = CHUNKS // 2
    for step in range(steps):
        for chunk in range(CHUNKS):
            multiply(step, chunk)
            if chunk < late:
                if step > 0:
                    finish(step - 1, late + chunk)
            else:
                finish(step, chunk - late)
            if chunk == 0 and step == 0:
                start_gather(2)
                start_gather(3)
            if chunk == late - 1 and step < steps - 1:
                make_operator(step + 1)
            if chunk == late and step + 3 <= steps:
                relay_gather(step + 3)
                if step == 0:
                    relay_gather(2)
        if step + 4 <= steps:
            start_gather(step + 4)
    for chunk in range(late, CHUNKS):
        finish(steps - 1, chunk)

    for step in range(steps):
        for chunk in range(CHUNKS):
            for which in range(3):
                part_copy(step, chunk, which).wait_send()
            if step >= top:
                result_copy(step, chunk).wait()

    @pl.when(has_high)
    def _():
        for step in range(steps):
            for chunk in range(CHUNKS):
                halo_copy(step, chunk, 0).wait_send()

    @pl.when(has_low)
    def _():
        for step in range(steps):
            for chunk in range(CHUNKS):
                halo_copy(step, chunk, 1).wait_send()

    for turn in range(steps + 1):
        for which in (0, 1, 4) if turn < DIRECT else (0, 1, 2, 3):
            gather_copy(turn, which).wait_send()


def on_device(
    right_side, lower_blocks, upper_blocks, lower_inverse, upper_inverse, lower_source, upper_source
):
    levels, nodes, order, columns = right_side.shape
    terms, part = lower_blocks.shape[2:4]
    rows = nodes * part
    steps = 2 * (levels - 1)
    wide = columns // CHUNKS
    sizes = (levels, nodes, terms, part, order, rows, columns)
    anywhere = pl.BlockSpec(memory_space=pl.ANY)
    scalars = pl.BlockSpec(memory_space=pltpu.SMEM)
    dma = pltpu.SemaphoreType.DMA
    return pl.pallas_call(
        functools.partial(kernel, sizes),
        out_shape=jax.ShapeDtypeStruct((levels, nodes, part, columns), BF16),
        in_specs=[anywhere] * 5 + [scalars] * 2,
        out_specs=anywhere,
        scratch_shapes=[
            pltpu.VMEM((nodes, part, order), BF16),
            pltpu.VMEM((nodes, order, columns), BF16),
            pltpu.VMEM((steps, nodes, terms, part, order), BF16),
            pltpu.VMEM((nodes, 4 * nodes, part, order), BF16),
            pltpu.VMEM((steps + 1, nodes, 4, part, order), BF16),
            pltpu.VMEM((steps, 4, nodes, part, 4 * nodes * part), BF16),
            pltpu.VMEM((steps + 1, CHUNKS, 4 * nodes, part, wide), BF16),
            pltpu.VMEM((CHUNKS, nodes, part, wide), F32),
            pltpu.VMEM((steps, CHUNKS, 3, nodes, part, wide), BF16),
            pltpu.VMEM((steps, CHUNKS, 3, nodes, part, wide), BF16),
            dma((steps + 1, CHUNKS, 2)),
            dma((steps + 1, CHUNKS, 2)),
            dma((steps, CHUNKS, 3)),
            dma((steps, CHUNKS, 3)),
            dma((steps + 1, 5)),
            dma((steps + 1, 5)),
            dma((2,)),
            dma((steps,)),
            dma((steps + 1,)),
            dma((levels - 1, CHUNKS)),
            dma((steps, CHUNKS)),
        ],
        compiler_params=pltpu.CompilerParams(
            collective_id=0, has_side_effects=True, vmem_limit_bytes=62 * 1024 * 1024
        ),
        cost_estimate=pl.CostEstimate(
            flops=4_000_000_000, bytes_accessed=10_000_000, transcendentals=0
        ),
        name="solve",
    )(
        right_side,
        lower_blocks,
        upper_blocks,
        lower_inverse,
        upper_inverse,
        lower_source,
        upper_source,
    )


def solution(mesh):
    placed = (
        P(None, "row", None, None),
        P(None, "row", None, "col", None),
        P(None, "row", None, "col", None),
        P(None, "row", "col", None),
        P(None, "row", "col", None),
        P(None, "row", None),
        P(None, "row", None),
    )
    return jax.shard_map(
        on_device,
        mesh=mesh,
        in_specs=placed,
        out_specs=P(None, "row", "col", None),
        check_vma=False,
    )
```
